256 devices in a mesh: expert: 4 (over y_lo, core), tensor: 64 (over x, y_hi, z).
Axes of the slice: x: 4, y: 4 (y_hi: 2, y_lo: 2; y = y_hi * 2 + y_lo), z: 8, core: 2. Of those that a mesh axis runs over, the one named last changes fastest.
Arguments:
- tokens: bfloat16 [1024, 6144], P('expert', 'tensor'), may hold values from -6 to 6
- expert_ids: int32 [1024, 2], P('expert'), may hold values from 0 to 3, all different within a row; in each aligned block of 256 rows (0 to 255, 256 to 511, ...) at most 192 rows name the same one
- route_gates: float32 [1024, 2], P('expert'), may hold values from 0.2 to 1
- w_gate: bfloat16 [4, 6144, 16384], P('expert', None, 'tensor'), may hold values from -0.078125 to 0.078125
- w_up: bfloat16 [4, 6144, 16384], P('expert', None, 'tensor'), may hold values from -0.078125 to 0.078125
- w_down: bfloat16 [4, 16384, 6144], P('expert', 'tensor'), may hold values from -0.125 to 0.125
Outputs:
- mixed: bfloat16 [1024, 6144], P('expert', 'tensor')
The draws below stay inside these ranges and needn't reach their ends.
Inputs may be any that keep to these rules, and one draw needn't show every extreme that they name: `expert_ids`: each token names two different experts; in each aligned block of 256 tokens no expert is named by more than 192 tokens, a bound that some block reaches.
All inputs are finite; a program needn't handle non-finite values.
Results may differ from the reference program's by a relative error of at most 0.012.
Values may be sent and summed in bfloat16 or wider, within the bound.
No kernel may reach another device: no remote copies, remote signals or barrier semaphores. Data moves between devices by JAX's collectives and lax.ppermute only.
A program may use at most 128 MiB of HBM per device.

```python
import math
import jax
import jax.numpy as jnp
import numpy as np

D = 6144
FF = 16384
TOK_GRP = 256
EXPERTS = 4
CAP = 192
TOKENS = 1024
N_EXPERT = 4


def spiked(drawn, rng, source, target, parts, factor):
    def block_of(axis_at):
        return (jnp.arange(drawn.shape[axis_at]) // (drawn.shape[axis_at] // parts)).reshape((-1,) + (1,) * (drawn.ndim - 1 - axis_at))

    first = jax.random.permutation(rng, parts)[block_of(target)]
    other_side = (block_of(target) + parts // 2) % parts
    return jnp.where((block_of(source) == first) | (block_of(source) == other_side), factor * drawn, drawn)


def levels(stream_key, dims, pieces, low, largest):
    def one(dim, shards_of):
        steps = jax.random.uniform(jax.random.fold_in(jax.random.fold_in(stream_key, 6), dim), (shards_of,), jnp.float32, low / len(pieces), largest / len(pieces))
        return jnp.repeat(jnp.exp(steps), dims[dim] // shards_of).reshape((-1,) + (1,) * (len(dims) - dim - 1))

    loudness = one(*pieces[0])
    for cut in pieces[1:]:
        loudness = loudness * one(*cut)
    return loudness


def shared_out(rng, own, number, rows, amount, top, reach, skew):
    ranking = jax.random.permutation(rng, amount)
    crowded, common = shares(amount, rows * top, reach, skew, True), shares(amount, rows * top, reach, skew, False)
    places = jnp.arange(amount)

    def named(tallies, turn):
        used = int((tallies > 0).sum())
        fixed = max(1, used // 4)
        moved = fixed + (places - fixed + turn * (used - fixed)) % max(1, amount - fixed)
        return jnp.zeros((amount,), jnp.int32).at[ranking[jnp.where(places < fixed, places, moved)]].set(jnp.asarray(tallies, jnp.int32))

    tallies = jnp.where(number % 4 == 0, named(crowded, number // 4), named(common, number - number // 4 - 1))
    mixed = jax.random.permutation(jax.random.fold_in(own, 3), amount)
    source_of, receiver = mixed[0:amount // 2 * 2:2], mixed[1:amount // 2 * 2:2]
    room = jnp.minimum(tallies[source_of] - 1, reach - tallies[receiver]) // 2
    room = jnp.where((source_of == ranking[0]) | (receiver == ranking[0]) | (tallies[receiver] == 0), 0, jnp.maximum(room, 0))
    moved = jax.random.randint(jax.random.fold_in(own, 4), (amount // 2,), 0, 1 << 20) % (room + 1)
    tallies = tallies.at[source_of].add(-moved).at[receiver].add(moved)
    members = jnp.searchsorted(jnp.cumsum(tallies), jnp.arange(rows * top), side="right").astype(jnp.int32)
    table = members.reshape(top, rows).T
    table = table[jax.random.permutation(jax.random.fold_in(own, 1), rows)]
    turn = jax.random.randint(jax.random.fold_in(own, 2), (rows, 1), 0, top)
    return jnp.take_along_axis(table, (jnp.arange(top)[None, :] + turn) % top, axis=1)


def shares(count, total, most, lean, full):
    loads = [(1 << 20) // math.isqrt(rank ** lean) + 1 for rank in range(1, count + 1)]
    largest = most if full else min(most, max(-(-total // count), total * loads[0] // sum(loads)))
    least = 1 if total - largest >= count - 1 else 0
    counts, rest = [largest] + [least] * (count - 1), total - largest - least * (count - 1)
    while rest > 0:
        candidates = [i for i in range(1, count) if counts[i] < largest] or [i for i in range(1, count) if counts[i] < most]
        pool, remaining = sum([loads[i] for i in candidates]), rest
        for i in candidates:
            addition = min(most - counts[i], max(1, remaining * loads[i] // pool), rest)
            counts[i] = counts[i] + addition
            rest = rest - addition
    return np.array(counts)


def gaussian(own_key, dims, deviation, reach, pieces=(), kind=jnp.bfloat16):
    values = jax.random.normal(own_key, dims, jnp.float32) * deviation
    if len(pieces) > 0:
        values = levels(own_key, dims, pieces, -0.22, 0.18) * values
    return jnp.clip(values, min=-reach, max=reach).astype(kind)


def heavy_noise(stream_key, shape, deviation, most, pieces, heavy, kind=jnp.bfloat16):
    entries = deviation * jax.random.normal(stream_key, shape, jnp.float32)
    if pieces:
        entries = entries * levels(stream_key, shape, pieces, -0.22, 0.18)
    return jnp.clip(spiked(entries, jax.random.fold_in(stream_key, 3), *heavy), -most, most).astype(kind)


def setup_inputs(seed: int = 0) -> dict:
    arg_keys = jax.random.split(jax.random.key(seed), 7)
    tokens = gaussian(arg_keys[0], (TOKENS, D), 1.0, 6.0, ((0, 4), (1, 64)))
    expert_ids_keys = jax.random.split(jax.random.fold_in(arg_keys[1], 1), TOKENS // TOK_GRP)
    expert_ids_turns = jax.random.permutation(jax.random.fold_in(arg_keys[1], 3), TOKENS // TOK_GRP)
    expert_ids = jax.vmap(lambda own, number: shared_out(jax.random.fold_in(arg_keys[1], 2), own, number, TOK_GRP, EXPERTS, 2, CAP, 2))(expert_ids_keys, expert_ids_turns).reshape((TOKENS, 2))
    route_gates = jnp.clip(0.2 + 0.8 * jax.random.uniform(arg_keys[2], (TOKENS, 2), jnp.float32) ** levels(arg_keys[2], (TOKENS, 2), ((0, 4),), -0.2, 0.2), 0.2, 1.0)
    w_gate = gaussian(arg_keys[3], (EXPERTS, D, FF), D ** -0.5, 0.078125, ((0, 4), (2, 64)))
    w_up = gaussian(arg_keys[4], (EXPERTS, D, FF), D ** -0.5, 0.078125, ((0, 4), (2, 64)))
    w_down = heavy_noise(arg_keys[5], (EXPERTS, FF, D), FF ** -0.5, 0.125, ((0, 4), (1, 64)), (1, 2, 64, 4.0))
    return {"tokens": tokens, "expert_ids": expert_ids, "route_gates": route_gates, "w_gate": w_gate, "w_up": w_up, "w_down": w_down}


def reference(tokens, expert_ids, route_gates, w_gate, w_up, w_down):
    total = tokens.shape[0]
    room = N_EXPERT * CAP
    accum = jnp.zeros((total, tokens.shape[1]), jnp.float32)
    for expert in range(EXPERTS):
        chosen = expert_ids == expert
        named = jnp.any(chosen, axis=1)
        share = jnp.sum(jnp.where(chosen, route_gates, 0.0), axis=1)
        position = (jnp.cumsum(named.astype(jnp.int32)) - 1).astype(jnp.int32)
        target = jnp.where(named, position, room).astype(jnp.int32)
        index = jnp.zeros((room,), jnp.int32).at[target].set(jnp.arange(total, dtype=jnp.int32), mode="drop")
        rows = tokens[index]
        gate = jnp.dot(rows, w_gate[expert], preferred_element_type=jnp.float32)
        up_rows = jnp.dot(rows, w_up[expert], preferred_element_type=jnp.float32)
        hidden = (jax.nn.silu(gate) * up_rows).astype(jnp.bfloat16)
        result = jnp.dot(hidden, w_down[expert], preferred_element_type=jnp.float32).astype(jnp.bfloat16)
        picked = result[jnp.where(named, position, 0).astype(jnp.int32)].astype(jnp.float32)
        accum = accum + share[:, None] * picked
    return accum.astype(jnp.bfloat16)
```

```python
import jax
import jax.numpy as jnp
from jax import lax
from jax.experimental import pallas as pl
from jax.experimental.pallas import tpu as pltpu
from jax.sharding import Mesh, PartitionSpec as P

AXES = ("ylo", "core", "x", "yhi", "z")
SIZES = (2, 2, 4, 2, 8)
NX, NZ = 4, 8
Y = ("ylo", "yhi")
BF16, F32 = jnp.bfloat16, jnp.float32
HALF = 128


def ring(n, s):
    return [(i, (i + s) % n) for i in range(n)]


def yring(s):
    idx = lambda y: (y % 2) * 2 + y // 2
    return [(idx(y), idx((y + s) % 4)) for y in range(4)]


def from_x(v, s):
    return lax.ppermute(v, "x", ring(NX, -s))


def from_z(v, s):
    return lax.ppermute(v, "z", ring(NZ, -s))


def from_y(v, s):
    return lax.ppermute(v, Y, yring(-s))


def sibling(v):
    return lax.ppermute(v, "core", [(0, 1), (1, 0)])


def dot(a, b):
    return lax.dot_general(a, b, (((1,), (0,)), ((), ())), preferred_element_type=F32)


def hidden_kernel(wg_ref, wu_ref, xa_ref, xb_ref, w_ref, h_ref, g_acc, u_acc):
    step = pl.program_id(0)
    x = jnp.concatenate([xa_ref[0], xa_ref[1], xb_ref[0], xb_ref[1]], axis=1)
    g = dot(wg_ref[...], x)
    u = dot(wu_ref[...], x)

    @pl.when(step == 0)
    def _():
        g_acc[...] = g
        u_acc[...] = u

    @pl.when(step > 0)
    def _():
        g_acc[...] += g
        u_acc[...] += u

    @pl.when(step == pl.num_programs(0) - 1)
    def _():
        g = g_acc[...]
        h_ref[...] = (g / (1.0 + jnp.exp(-g)) * u_acc[...] * w_ref[...]).astype(BF16)


def hidden_of(wg_t, wu_t, xa, xb, w):
    ff, d = wg_t.shape
    kb = d // 4
    return pl.pallas_call(
        hidden_kernel,
        grid=(d // kb,),
        in_specs=[
            pl.BlockSpec((ff, kb), lambda k: (0, k)),
            pl.BlockSpec((ff, kb), lambda k: (0, k)),
            pl.BlockSpec((2, kb, HALF), lambda k: (0, k, 0)),
            pl.BlockSpec((2, kb, HALF), lambda k: (0, k, 0)),
            pl.BlockSpec((1, 4 * HALF), lambda k: (0, 0)),
        ],
        out_specs=pl.BlockSpec((ff, 4 * HALF), lambda k: (0, 0)),
        out_shape=jax.ShapeDtypeStruct((ff, 4 * HALF), BF16),
        scratch_shapes=[pltpu.VMEM((ff, 4 * HALF), F32), pltpu.VMEM((ff, 4 * HALF), F32)],
        compiler_params=pltpu.CompilerParams(vmem_limit_bytes=24 * 1024 * 1024),
    )(wg_t, wu_t, xa, xb, w)


def down_kernel(wd_ref, h_ref, oa_ref, ob_ref):
    o = dot(wd_ref[...], h_ref[...]).astype(BF16)
    for i, ref in enumerate((oa_ref, ob_ref)):
        for j in range(2):
            k = (2 * i + j) * HALF
            ref[j] = o[:, k : k + HALF]


def down_of(wd_t, h):
    d, ff = wd_t.shape
    rb = d // 4
    part = jax.ShapeDtypeStruct((2, d, HALF), BF16)
    return pl.pallas_call(
        down_kernel,
        grid=(d // rb,),
        in_specs=[
            pl.BlockSpec((rb, ff), lambda r: (r, 0)),
            pl.BlockSpec((ff, 4 * HALF), lambda r: (0, 0)),
        ],
        out_specs=[pl.BlockSpec((2, rb, HALF), lambda r: (0, r, 0))] * 2,
        out_shape=[part, part],
        compiler_params=pltpu.CompilerParams(vmem_limit_bytes=24 * 1024 * 1024),
    )(wd_t, h)


def put(buf, piece, *at):
    zero = jnp.int32(0)
    at = tuple(jnp.asarray(a, jnp.int32) for a in at) + (zero,) * (buf.ndim - len(at))
    return lax.dynamic_update_slice(buf, piece, at)


def take(buf, sizes, *at):
    zero = jnp.int32(0)
    at = tuple(jnp.asarray(a, jnp.int32) for a in at) + (zero,) * (buf.ndim - len(at))
    return lax.dynamic_slice(buf, at, sizes)


def add(*vs):
    total = vs[0].astype(F32)
    for v in vs[1:]:
        total = total + v.astype(F32)
    return total.astype(BF16)


def body(tokens, expert_ids, route_gates, w_gate, w_up, w_down):
    feats = tokens.shape[1]
    rows = NZ * feats
    ylo, core, x, yhi, z = (lax.axis_index(a) for a in AXES)
    y = 2 * yhi + ylo

    wg_t, wu_t, wd_t = w_gate[0].T, w_up[0].T, w_down[0].T

    experts = jnp.arange(4, dtype=jnp.int32)
    mine = jnp.sum(
        jnp.where(expert_ids[None, :, :] == experts[:, None, None], route_gates[None], 0.0), axis=2
    )
    pair = jnp.stack([mine, sibling(mine)])
    other = lax.ppermute(pair, "ylo", [(0, 1), (1, 0)])
    share = lambda v: lax.dynamic_index_in_dim(v, 2 * ylo + core, axis=1, keepdims=False)
    pair, other = share(pair), share(other)
    low, high = jnp.where(ylo == 0, pair, other), jnp.where(ylo == 0, other, pair)
    w_own, w_sib = (
        jnp.concatenate([low[i, :HALF], high[i, :HALF], low[i, HALF:], high[i, HALF:]])[None]
        for i in (0, 1)
    )

    own = tokens.T
    pieces = [own] + [from_z(own, s) for s in range(1, NZ)]
    start = [jnp.zeros((NZ, feats, HALF), BF16) for _ in range(2)]
    for s, piece in enumerate(pieces):
        for i in range(2):
            start[i] = put(start[i], piece[None, :, i * HALF : (i + 1) * HALF], (z + s) % NZ)
    a1, b1 = (v.reshape(rows, HALF) for v in start)

    def spot(s):
        return ((y + s) % 4) % 2, ((y + s) % 4) // 2

    a2 = jnp.zeros((2, 2, rows, HALF), BF16)
    for s, piece in ((0, a1), (1, from_y(a1, 1)), (3, from_y(a1, -1)), (2, from_y(a1, 2))):
        a2 = put(a2, piece[None, None], *spot(s))
    a2 = a2.reshape(2, 1, 2 * rows, HALF)
    right, left = from_x(a2, 1), from_x(a2, -1)
    far0, far1 = from_x(right[0:1], 1), from_x(left[1:2], -1)
    a3 = jnp.zeros((2, NX, 2 * rows, HALF), BF16)
    a3 = put(a3, a2, 0, x)
    a3 = put(a3, right, 0, (x + 1) % NX)
    a3 = put(a3, left, 0, (x + 3) % NX)
    a3 = put(a3, far0, 0, (x + 2) % NX)
    a3 = put(a3, far1, 1, (x + 2) % NX)
    xa = a3.reshape(2, NX * 2 * rows, HALF)

    b2 = jnp.zeros((NX, rows, HALF), BF16)
    for s, piece in ((0, b1), (1, from_x(b1, 1)), (3, from_x(b1, -1)), (2, from_x(b1, 2))):
        b2 = put(b2, piece[None], (x + s) % NX)
    right, left = from_y(b2, 1), from_y(b2, -1)
    far0, far1 = from_y(right[0:2], 1), from_y(left[2:4], -1)
    b3 = jnp.zeros((2, NX, 2, rows, HALF), BF16)
    for s, at, piece in ((0, 0, b2), (1, 0, right), (3, 0, left), (2, 0, far0), (2, 2, far1)):
        ylo_s, yhi_s = spot(s)
        b3 = put(b3, piece[None, :, None], ylo_s, at, yhi_s)
    xb = b3.reshape(2, NX * 2 * rows, HALF)

    xa_sib, xb_sib = sibling(xa), sibling(xb)

    h_own = hidden_of(wg_t, wu_t, xa, xb, w_own)
    h_sib = hidden_of(wg_t, wu_t, xa_sib, xb_sib, w_sib)
    pa_sib, pb_sib = down_of(wd_t, h_sib)
    pa, pb = down_of(wd_t, h_own)
    ra, rb = sibling(pa_sib), sibling(pb_sib)

    def chunk(s):
        size = (2, 1, 2 * rows, HALF)
        at = (0, (x + s) % NX)
        shape = (2, NX, 2 * rows, HALF)
        return take(pa.reshape(shape), size, *at), take(ra.reshape(shape), size, *at)

    far = add(*chunk(2))
    got0, got1 = from_x(far[0:1], -1), from_x(far[1:2], 1)
    p, r = chunk(1)
    to_right = jnp.concatenate([add(p[0:1], r[0:1], got0), add(p[1:2], r[1:2])])
    p, r = chunk(3)
    to_left = jnp.concatenate([add(p[0:1], r[0:1]), add(p[1:2], r[1:2], got1)])
    sa = add(*chunk(0), from_x(to_right, -1), from_x(to_left, 1)).reshape(2, 2, rows, HALF)
    ychunk = lambda s: take(sa, (1, 1, rows, HALF), *spot(s)).reshape(rows, HALF)
    sa = add(ychunk(0), *[from_y(ychunk(s), -s) for s in (1, 3, 2)])

    def chunk_b(s):
        size = (1, NX, 1, rows, HALF)
        ylo_s, yhi_s = spot(s)
        shape = (2, NX, 2, rows, HALF)
        return tuple(
            take(v.reshape(shape), size, ylo_s, 0, yhi_s).reshape(NX, rows, HALF) for v in (pb, rb)
        )

    far = add(*chunk_b(2))
    got0, got1 = from_y(far[0:2], -1), from_y(far[2:4], 1)
    p, r = chunk_b(1)
    to_right = jnp.concatenate([add(p[0:2], r[0:2], got0), add(p[2:4], r[2:4])])
    p, r = chunk_b(3)
    to_left = jnp.concatenate([add(p[0:2], r[0:2]), add(p[2:4], r[2:4], got1)])
    sb = add(*chunk_b(0), from_y(to_right, -1), from_y(to_left, 1))
    xchunk = lambda s: take(sb, (1, rows, HALF), (x + s) % NX).reshape(rows, HALF)
    sb = add(xchunk(0), *[from_x(xchunk(s), -s) for s in (1, 3, 2)])

    both = jnp.concatenate([sa, sb], axis=1).reshape(NZ, feats, 2 * HALF)
    zchunk = lambda s: take(both, (1, feats, 2 * HALF), (z + s) % NZ)[0]
    mixed = add(zchunk(0), *[from_z(zchunk(s), -s) for s in range(1, NZ)])
    return mixed.T


def solution(mesh):
    fine = Mesh(mesh.devices.reshape(SIZES), AXES)
    expert, tensor = ("ylo", "core"), ("x", "yhi", "z")
    in_specs = (
        P(expert, tensor),
        P(expert, None),
        P(expert, None),
        P(expert, None, tensor),
        P(expert, None, tensor),
        P(expert, tensor, None),
    )
    return jax.shard_map(
        body, mesh=fine, in_specs=in_specs, out_specs=P(expert, tensor), check_vma=False
    )
```

```python
import itertools

import jax
import jax.numpy as jnp
from jax import lax
from jax.experimental import pallas as pl
from jax.experimental.pallas import tpu as pltpu
from jax.sharding import Mesh, PartitionSpec as P

AXES = ("ylo", "core", "x", "yhi", "z")
SIZES = (2, 2, 4, 2, 8)
NZ = 8
BF16, F32 = jnp.bfloat16, jnp.float32
COLS = 256


def flat(ylo, core, x, yhi, z):
    return (((ylo * 2 + core) * 4 + x) * 2 + yhi) * 8 + z


def shift_perm(major, s):
    pairs = []
    for ylo, core, x, yhi, z in itertools.product(*map(range, SIZES)):
        if (core == 0) == major:
            source = flat(ylo, core, (x + s) % 4, yhi, z)
        else:
            y = (2 * yhi + ylo + s) % 4
            source = flat(y % 2, core, x, y // 2, z)
        pairs.append((source, flat(ylo, core, x, yhi, z)))
    return pairs


def from_major(v, s):
    return lax.ppermute(v, AXES, shift_perm(True, s))


def from_minor(v, s):
    return lax.ppermute(v, AXES, shift_perm(False, s))


def from_z(v, s):
    return lax.ppermute(v, "z", [((i + s) % NZ, i) for i in range(NZ)])


def z_pair(v):
    return lax.ppermute(v, "z", [(i, i ^ 1) for i in range(NZ)])


def sibling(v):
    return lax.ppermute(v, "core", [(0, 1), (1, 0)])


def dot_t(a, b):
    return lax.dot_general(a, b, (((0,), (0,)), ((), ())), preferred_element_type=F32)


def place(at, i, j, other):
    across = (at[2] == 0) != bool(other)
    dx, dy = jnp.where(across, i, j), jnp.where(across, j, i)
    block = lax.rem(at[0] + dx, 4) * 2 + lax.div(lax.rem(at[1] + dy, 4), 2)
    return block, lax.rem(dy, 2)


OWN = ((0, 0), (0, 1), (0, 2), (0, 3))
THROUGH = ((1, 0), (1, 1), (3, 2), (3, 3))
DIRECT = ((1, 2), (1, 3), (3, 0), (3, 1))
FAR = ((2, 0), (2, 1), (2, 2), (2, 3))


def block_at(at, blocks, t, other):
    def select(values):
        out = jnp.int32(values[0])
        for k, v in enumerate(values[1:], 1):
            out = jnp.where(t == k, v, out)
        return out

    i, j = zip(*blocks)
    return place(at, select(i), select(j), other)


def half_specs(rows, n):
    def spec(k):
        return pl.BlockSpec((1, rows, COLS), lambda t, at: (jnp.clip(t - 2 * k, 0, 1), 0, 0))

    return [spec(k) for k in range(n)]


def hidden_kernel(blocks, first, last, at, wg0, wu0, wg1, wu1, *refs):
    t, n = pl.program_id(0), len(blocks) // 2
    own, theirs, refs = refs[:n], refs[n : 2 * n], refs[2 * n :]
    if not first:
        before, refs = refs[0], refs[1:]
    if last:
        w_ref, h_ref, acc = refs
    else:
        (acc,) = refs

    @pl.when(t == 0)
    def _():
        acc[...] = jnp.zeros_like(acc) if first else before[...]

    for k, pair in enumerate(zip(own, theirs)):

        @pl.when(lax.div(t, 2) == k)
        def _(pair=pair):
            for part, (ref, wg, wu) in enumerate(zip(pair, (wg0, wg1), (wu0, wu1))):
                _, group = block_at(at, blocks, t, part)
                v = ref[0]
                acc[part, group, 0] += dot_t(wg[...], v)
                acc[part, group, 1] += dot_t(wu[...], v)

    if last:

        @pl.when(t == len(blocks) - 1)
        def _():
            for part in range(2):
                for group in range(2):
                    g, u = acc[part, group, 0], acc[part, group, 1]
                    h = g / (1.0 + jnp.exp(-g)) * u * w_ref[part, group]
                    h_ref[part, group] = h.astype(BF16)


def hidden_of(at, wg, wu, blocks, own, theirs, before=None, w=None):
    d, ff = wg.shape
    rows = d // 8
    sums = (2, 2, 2, ff, COLS)

    def weights(part):
        return pl.BlockSpec((rows, ff), lambda t, at: (block_at(at, blocks, t, part)[0], 0))

    whole = lambda shape: pl.BlockSpec(shape, lambda t, at: (0,) * len(shape))
    in_specs = [weights(0)] * 2 + [weights(1)] * 2 + half_specs(rows, len(own)) * 2
    args = [wg, wu, wg, wu, *own, *theirs]
    if before is not None:
        in_specs.append(whole(sums))
        args.append(before)
    if w is not None:
        in_specs.append(whole((2, 2, 1, COLS)))
        args.append(w)
        out = (2, 2, ff, COLS)
        out_specs, out_shape = whole(out), jax.ShapeDtypeStruct(out, BF16)
        scratch = [pltpu.VMEM(sums, F32)]
    else:
        out_specs, out_shape, scratch = whole(sums), jax.ShapeDtypeStruct(sums, F32), []

    def kernel(*refs):
        hidden_kernel(blocks, before is None, w is not None, *refs)

    return pl.pallas_call(
        kernel,
        grid_spec=pltpu.PrefetchScalarGridSpec(
            num_scalar_prefetch=1,
            grid=(len(blocks),),
            in_specs=in_specs,
            out_specs=out_specs,
            scratch_shapes=scratch,
        ),
        out_shape=out_shape,
        compiler_params=pltpu.CompilerParams(vmem_limit_bytes=24 * 1024 * 1024),
    )(at, *args)


def down_kernel(keep, at, wd_ref, h_ref, *refs):
    t = pl.program_id(0)
    o = dot_t(wd_ref[...], h_ref[0, 0])
    if not keep:
        refs[0][0] = o.astype(BF16)
        return
    o = o + refs[0][0].astype(F32)
    via, outs = refs[1:-2], refs[-2:]
    for k, ref in enumerate(outs):

        @pl.when(lax.div(t, 2) == k)
        def _(k=k, ref=ref):
            ref[0] = (o + via[k][0].astype(F32) if via else o).astype(BF16)


def down_of(at, wd, h, blocks, got=None, first=0, via=()):
    ff, d = wd.shape
    rows = d // 8
    part = 1 if got is None else 0
    whole = pl.BlockSpec((1, rows, COLS), lambda t, at: (t + first, 0, 0))
    in_specs = [
        pl.BlockSpec((ff, rows), lambda t, at: (0, block_at(at, blocks, t, part)[0])),
        pl.BlockSpec((1, 1, ff, COLS), lambda t, at: (part, block_at(at, blocks, t, part)[1], 0, 0)),
    ]
    args = [wd, h]
    if got is None:
        out_specs, out_shape = whole, jax.ShapeDtypeStruct((len(blocks), rows, COLS), BF16)
    else:
        in_specs += [whole, *half_specs(rows, len(via))]
        args += [got, *via]
        out_specs, out_shape = half_specs(rows, 2), [jax.ShapeDtypeStruct((2, rows, COLS), BF16)] * 2

    def kernel(*refs):
        down_kernel(got is not None, *refs)

    return pl.pallas_call(
        kernel,
        grid_spec=pltpu.PrefetchScalarGridSpec(
            num_scalar_prefetch=1, grid=(len(blocks),), in_specs=in_specs, out_specs=out_specs
        ),
        out_shape=out_shape,
        compiler_params=pltpu.CompilerParams(vmem_limit_bytes=12 * 1024 * 1024),
    )(at, *args)


def at_index(i, ndim):
    return (jnp.asarray(i, jnp.int32),) + (jnp.int32(0),) * (ndim - 1)


def put(buf, piece, i):
    return lax.dynamic_update_slice(buf, piece, at_index(i, buf.ndim))


def take(buf, i):
    return lax.dynamic_slice(buf, at_index(i, buf.ndim), (1,) + buf.shape[1:])[0]


def total(*vs):
    out = vs[0].astype(F32)
    for v in vs[1:]:
        out = out + v.astype(F32)
    return out.astype(BF16)


def body(tokens, expert_ids, route_gates, w_gate, w_up, w_down):
    feats = tokens.shape[1]
    rows = NZ * feats
    ylo, core, x, yhi, z = (lax.axis_index(a).astype(jnp.int32) for a in AXES)
    zh, zl = z // 2, z % 2
    at = jnp.stack([x, 2 * yhi + ylo, core])
    wg, wu, wd = w_gate[0], w_up[0], w_down[0]

    own = tokens.T
    pair = z_pair(own)
    pair = jnp.stack([jnp.where(zl == 0, own, pair), jnp.where(zl == 0, pair, own)])
    start = jnp.zeros((NZ // 2, 2, feats, COLS), BF16)
    for s in range(NZ // 2):
        piece = from_z(pair, 2 * s) if s else pair
        start = put(start, piece[None], (zh + s) % 4)
    start = start.reshape(rows, COLS)

    experts = jnp.arange(4, dtype=jnp.int32)
    mine = jnp.sum(
        jnp.where(expert_ids[None, :, :] == experts[:, None, None], route_gates[None], 0.0), axis=2
    )
    near = jnp.stack([mine, sibling(mine)])
    other = lax.ppermute(near, "ylo", [(0, 1), (1, 0)])
    w = jnp.stack([near, other], axis=1)
    w = lax.dynamic_index_in_dim(w, 2 * ylo + core, axis=2)

    steps = {s: from_minor(start, s) for s in (1, 2, 3)}
    own = [jnp.stack([start, steps[1]]), jnp.stack([steps[2], steps[3]])]
    *own, w = lax.optimization_barrier((*own, w))

    through = [from_major(own[0], 1), from_major(own[1], 3)]
    direct = [from_major(own[1], 1), from_major(own[0], 3)]
    far = [from_major(through[0], 1), from_major(through[1], 3)]
    swap = lambda vs: [sibling(v) for v in vs]
    sums = hidden_of(at, wg, wu, OWN, own, swap(own))
    *near, sums = lax.optimization_barrier((*through, *direct, sums))
    sums = hidden_of(at, wg, wu, THROUGH + DIRECT, near, swap(near), sums)
    *far, sums = lax.optimization_barrier((*far, sums))
    h = hidden_of(at, wg, wu, FAR, far, swap(far), sums, w)

    def after(h, v):
        return lax.optimization_barrier((h, v))

    h, p = after(h, down_of(at, wd, h, FAR))
    got = sibling(p)
    h, give, rest = lax.optimization_barrier((h, down_of(at, wd, h, DIRECT), down_of(at, wd, h, THROUGH + OWN)))
    h, got = after(h, got)
    far = down_of(at, wd, h, FAR, got)
    h, give, rest, *far = lax.optimization_barrier((h, give, rest, *far))
    via = [from_major(far[0], 3), from_major(far[1], 1)]
    h, got = after(h, sibling(give))
    direct = down_of(at, wd, h, DIRECT, got)
    direct = [from_major(direct[0], 3), from_major(direct[1], 1)]
    got = sibling(rest)
    h, *moved = lax.optimization_barrier((h, *via, *direct))
    via, direct = moved[:2], moved[2:]
    h, through = after(h, down_of(at, wd, h, THROUGH, got, 0, via))
    through = [from_major(through[0], 3), from_major(through[1], 1)]
    own = down_of(at, wd, h, OWN, got, 4)
    low = [total(own[0][j], through[0][j], direct[1][j]) for j in range(2)]
    high = [total(own[1][j], direct[0][j], through[1][j]) for j in range(2)]

    c = [*low, *high]
    came = {s: from_minor(c[s], -s) for s in (2, 1, 3)}
    c = total(c[0], came[1], came[3], came[2])

    c = c.reshape(NZ // 2, 2, feats, COLS)
    chunk = lambda s: take(c, (zh + s) % 4)
    c = total(chunk(0), *[from_z(chunk(s), -2 * s) for s in (2, 1, 3)])
    c = total(take(c, zl), z_pair(take(c, 1 - zl)))
    return c.T


def solution(mesh):
    fine = Mesh(mesh.devices.reshape(SIZES), AXES)
    expert, tensor = ("ylo", "core"), ("x", "yhi", "z")
    in_specs = (
        P(expert, tensor),
        P(expert, None),
        P(expert, None),
        P(expert, None, tensor),
        P(expert, None, tensor),
        P(expert, tensor, None),
    )
    return jax.shard_map(
        body, mesh=fine, in_specs=in_specs, out_specs=P(expert, tensor), check_vma=False
    )
```

```python
import itertools

import jax
import jax.numpy as jnp
from jax import lax
from jax.experimental import pallas as pl
from jax.experimental.pallas import tpu as pltpu
from jax.sharding import Mesh, PartitionSpec as P

AXES = ("ylo", "core", "x", "yhi", "z")
SIZES = (2, 2, 4, 2, 8)
NZ = 8
BF16, F32 = jnp.bfloat16, jnp.float32
COLS = 256


def flat(ylo, core, x, yhi, z):
    return (((ylo * 2 + core) * 4 + x) * 2 + yhi) * 8 + z


def shift_perm(major, s):
    pairs = []
    for ylo, core, x, yhi, z in itertools.product(*map(range, SIZES)):
        if (core == 0) == major:
            source = flat(ylo, core, (x + s) % 4, yhi, z)
        else:
            y = (2 * yhi + ylo + s) % 4
            source = flat(y % 2, core, x, y // 2, z)
        pairs.append((source, flat(ylo, core, x, yhi, z)))
    return pairs


def from_major(v, s):
    return lax.ppermute(v, AXES, shift_perm(True, s))


def from_minor(v, s):
    return lax.ppermute(v, AXES, shift_perm(False, s))


def from_z(v, s):
    return lax.ppermute(v, "z", [((i + s) % NZ, i) for i in range(NZ)])


def z_pair(v):
    return lax.ppermute(v, "z", [(i, i ^ 1) for i in range(NZ)])


def sibling(v):
    return lax.ppermute(v, "core", [(0, 1), (1, 0)])


def dot_t(a, b):
    return lax.dot_general(a, b, (((0,), (0,)), ((), ())), preferred_element_type=F32)


def place(at, i, j, other):
    across = (at[2] == 0) != bool(other)
    dx, dy = jnp.where(across, i, j), jnp.where(across, j, i)
    block = lax.rem(at[0] + dx, 4) * 2 + lax.div(lax.rem(at[1] + dy, 4), 2)
    return block, lax.rem(dy, 2)


OWN = ((0, 0), (0, 1), (0, 2), (0, 3))
THROUGH = ((1, 0), (1, 1), (3, 2), (3, 3))
DIRECT = ((1, 2), (1, 3), (3, 0), (3, 1))
FAR = ((2, 0), (2, 1), (2, 2), (2, 3))


def block_at(at, blocks, t, other):
    def select(values):
        out = jnp.int32(values[0])
        for k, v in enumerate(values[1:], 1):
            out = jnp.where(t == k, v, out)
        return out

    i, j = zip(*blocks)
    return place(at, select(i), select(j), other)


def half_specs(rows, n):
    def spec(k):
        return pl.BlockSpec((1, rows, COLS), lambda t, at: (jnp.clip(t - 2 * k, 0, 1), 0, 0))

    return [spec(k) for k in range(n)]


def hidden_kernel(blocks, first, last, at, wg0, wu0, wg1, wu1, *refs):
    t, n = pl.program_id(0), len(blocks) // 2
    own, theirs, refs = refs[:n], refs[n : 2 * n], refs[2 * n :]
    if not first:
        before, refs = refs[0], refs[1:]
    if last:
        w_ref, h_ref, acc = refs
    else:
        (acc,) = refs

    @pl.when(t == 0)
    def _():
        acc[...] = jnp.zeros_like(acc) if first else before[...]

    for k, pair in enumerate(zip(own, theirs)):

        @pl.when(lax.div(t, 2) == k)
        def _(pair=pair):
            for part, (ref, wg, wu) in enumerate(zip(pair, (wg0, wg1), (wu0, wu1))):
                _, group = block_at(at, blocks, t, part)
                v = ref[0]
                acc[part, group, 0] += dot_t(wg[...], v)
                acc[part, group, 1] += dot_t(wu[...], v)

    if last:

        @pl.when(t == len(blocks) - 1)
        def _():
            for part in range(2):
                for group in range(2):
                    g, u = acc[part, group, 0], acc[part, group, 1]
                    h = g / (1.0 + jnp.exp(-g)) * u * w_ref[part, group]
                    h_ref[part, group] = h.astype(BF16)


def hidden_of(at, wg, wu, blocks, own, theirs, before=None, w=None):
    d, ff = wg.shape
    rows = d // 8
    sums = (2, 2, 2, ff, COLS)

    def weights(part):
        return pl.BlockSpec((rows, ff), lambda t, at: (block_at(at, blocks, t, part)[0], 0))

    whole = lambda shape: pl.BlockSpec(shape, lambda t, at: (0,) * len(shape))
    in_specs = [weights(0)] * 2 + [weights(1)] * 2 + half_specs(rows, len(own)) * 2
    args = [wg, wu, wg, wu, *own, *theirs]
    if before is not None:
        in_specs.append(whole(sums))
        args.append(before)
    if w is not None:
        in_specs.append(whole((2, 2, 1, COLS)))
        args.append(w)
        out = (2, 2, ff, COLS)
        out_specs, out_shape = whole(out), jax.ShapeDtypeStruct(out, BF16)
        scratch = [pltpu.VMEM(sums, F32)]
    else:
        out_specs, out_shape, scratch = whole(sums), jax.ShapeDtypeStruct(sums, F32), []

    def kernel(*refs):
        hidden_kernel(blocks, before is None, w is not None, *refs)

    return pl.pallas_call(
        kernel,
        grid_spec=pltpu.PrefetchScalarGridSpec(
            num_scalar_prefetch=1,
            grid=(len(blocks),),
            in_specs=in_specs,
            out_specs=out_specs,
            scratch_shapes=scratch,
        ),
        out_shape=out_shape,
        compiler_params=pltpu.CompilerParams(vmem_limit_bytes=24 * 1024 * 1024),
    )(at, *args)


def down_kernel(keep, via_n, at, wd_ref, h_ref, *refs):
    t = pl.program_id(0)
    o = dot_t(wd_ref[...], h_ref[0, 0])
    if not keep:
        refs[0][0] = o.astype(BF16)
        return
    o = o + refs[0][0].astype(F32)
    if via_n:
        via, outs = refs[1 : 1 + via_n], refs[1 + via_n :]
        o = o + jnp.where(t < 2, via[0][0], via[1][0]).astype(F32)
        for k, ref in enumerate(outs):

            @pl.when(t == k)
            def _(ref=ref):
                ref[0] = o.astype(BF16)

        return
    for k, ref in enumerate(refs[1:]):

        @pl.when(lax.div(t, 2) == k)
        def _(ref=ref):
            ref[0] = o.astype(BF16)


def down_of(at, wd, h, blocks, got=None, first=0, via=()):
    ff, d = wd.shape
    rows = d // 8
    part = 1 if got is None else 0
    whole = pl.BlockSpec((1, rows, COLS), lambda t, at: (t + first, 0, 0))
    in_specs = [
        pl.BlockSpec((ff, rows), lambda t, at: (0, block_at(at, blocks, t, part)[0])),
        pl.BlockSpec((1, 1, ff, COLS), lambda t, at: (part, block_at(at, blocks, t, part)[1], 0, 0)),
    ]
    args = [wd, h]
    if got is None:
        out_specs, out_shape = whole, jax.ShapeDtypeStruct((len(blocks), rows, COLS), BF16)
    else:
        in_specs += [whole, *half_specs(rows, len(via))]
        args += [got, *via]
        out_specs, out_shape = half_specs(rows, 2), [jax.ShapeDtypeStruct((2, rows, COLS), BF16)] * 2
        if via:
            out_specs = [pl.BlockSpec((1, rows, COLS), lambda t, at: (0, 0, 0))] * 4
            out_shape = [jax.ShapeDtypeStruct((1, rows, COLS), BF16)] * 4

    def kernel(*refs):
        down_kernel(got is not None, len(via), *refs)

    return pl.pallas_call(
        kernel,
        grid_spec=pltpu.PrefetchScalarGridSpec(
            num_scalar_prefetch=1, grid=(len(blocks),), in_specs=in_specs, out_specs=out_specs
        ),
        out_shape=out_shape,
        compiler_params=pltpu.CompilerParams(vmem_limit_bytes=12 * 1024 * 1024),
    )(at, *args)


def join_kernel(a, b, c, d, low, high):
    for out, pair in ((low, (a, b)), (high, (c, d))):
        for i, v in enumerate(pair):
            out[i] = v[...]


def join(*pieces):
    out = jax.ShapeDtypeStruct((2, *pieces[0].shape), BF16)
    return pl.pallas_call(
        join_kernel,
        out_shape=[out, out],
        compiler_params=pltpu.CompilerParams(vmem_limit_bytes=10 * 1024 * 1024),
    )(*pieces)


def at_index(i, ndim):
    return (jnp.asarray(i, jnp.int32),) + (jnp.int32(0),) * (ndim - 1)


def put(buf, piece, i):
    return lax.dynamic_update_slice(buf, piece, at_index(i, buf.ndim))


def take(buf, i):
    return lax.dynamic_slice(buf, at_index(i, buf.ndim), (1,) + buf.shape[1:])[0]


def total(*vs):
    out = vs[0].astype(F32)
    for v in vs[1:]:
        out = out + v.astype(F32)
    return out.astype(BF16)


def body(tokens, expert_ids, route_gates, w_gate, w_up, w_down):
    feats = tokens.shape[1]
    rows = NZ * feats
    ylo, core, x, yhi, z = (lax.axis_index(a).astype(jnp.int32) for a in AXES)
    zh, zl = z // 2, z % 2
    at = jnp.stack([x, 2 * yhi + ylo, core])
    wg, wu, wd = w_gate[0], w_up[0], w_down[0]

    own = tokens.T
    pair = z_pair(own)
    pair = jnp.stack([jnp.where(zl == 0, own, pair), jnp.where(zl == 0, pair, own)])
    start = jnp.zeros((NZ // 2, 2, feats, COLS), BF16)
    for s in range(NZ // 2):
        piece = from_z(pair, 2 * s) if s else pair
        start = put(start, piece[None], (zh + s) % 4)
    start = start.reshape(rows, COLS)

    experts = jnp.arange(4, dtype=jnp.int32)
    mine = jnp.sum(
        jnp.where(expert_ids[None, :, :] == experts[:, None, None], route_gates[None], 0.0), axis=2
    )
    near = jnp.stack([mine, sibling(mine)])
    other = lax.ppermute(near, "ylo", [(0, 1), (1, 0)])
    w = jnp.stack([near, other], axis=1)
    w = lax.dynamic_index_in_dim(w, 2 * ylo + core, axis=2)

    steps = {s: from_minor(start, s) for s in (1, 2, 3)}
    own = join(start, steps[1], steps[2], steps[3])
    *own, w = lax.optimization_barrier((*own, w))

    through = [from_major(own[0], 1), from_major(own[1], 3)]
    direct = [from_major(own[1], 1), from_major(own[0], 3)]
    far = [from_major(through[0], 1), from_major(through[1], 3)]
    swap = lambda vs: [sibling(v) for v in vs]
    sums = hidden_of(at, wg, wu, OWN, own, swap(own))
    *near, sums = lax.optimization_barrier((*through, *direct, sums))
    sums = hidden_of(at, wg, wu, THROUGH + DIRECT, near, swap(near), sums)
    *far, sums = lax.optimization_barrier((*far, sums))
    h = hidden_of(at, wg, wu, FAR, far, swap(far), sums, w)

    def after(h, v):
        return lax.optimization_barrier((h, v))

    h, p = after(h, down_of(at, wd, h, FAR))
    got = sibling(p)
    h, give, rest = lax.optimization_barrier((h, down_of(at, wd, h, DIRECT), down_of(at, wd, h, THROUGH + OWN)))
    h, got = after(h, got)
    far = down_of(at, wd, h, FAR, got)
    h, give, rest, *far = lax.optimization_barrier((h, give, rest, *far))
    via = [from_major(far[0], 3), from_major(far[1], 1)]
    h, got = after(h, sibling(give))
    direct = down_of(at, wd, h, DIRECT, got)
    direct = [from_major(direct[0], 3), from_major(direct[1], 1)]
    got = sibling(rest)
    h, through = after(h, down_of(at, wd, h, THROUGH, got, 0, via))
    through = [from_major(v, s) for v, s in zip(through, (3, 3, 1, 1))]
    own = down_of(at, wd, h, OWN, got, 4)
    low = [total(own[0][j], through[j][0], direct[1][j]) for j in range(2)]
    high = [total(own[1][j], direct[0][j], through[2 + j][0]) for j in range(2)]

    c = [*low, *high]
    came = {s: from_minor(c[s], -s) for s in (2, 1, 3)}
    c = total(c[0], came[1], came[3], came[2])

    c = c.reshape(NZ // 2, 2, feats, COLS)
    chunk = lambda s: take(c, (zh + s) % 4)
    c = total(chunk(0), *[from_z(chunk(s), -2 * s) for s in (2, 1, 3)])
    c = total(take(c, zl), z_pair(take(c, 1 - zl)))
    return c.T


def solution(mesh):
    fine = Mesh(mesh.devices.reshape(SIZES), AXES)
    expert, tensor = ("ylo", "core"), ("x", "yhi", "z")
    in_specs = (
        P(expert, tensor),
        P(expert, None),
        P(expert, None),
        P(expert, None, tensor),
        P(expert, None, tensor),
        P(expert, tensor, None),
    )
    return jax.shard_map(
        body, mesh=fine, in_specs=in_specs, out_specs=P(expert, tensor), check_vma=False
    )
```

```python
import itertools

import jax
import jax.numpy as jnp
from jax import lax
from jax.experimental import pallas as pl
from jax.experimental.pallas import tpu as pltpu
from jax.sharding import Mesh, PartitionSpec as P

AXES = ("ylo", "core", "x", "yhi", "z")
SIZES = (2, 2, 4, 2, 8)
NZ = 8
BF16, F32 = jnp.bfloat16, jnp.float32
COLS = 256


def flat(ylo, core, x, yhi, z):
    return (((ylo * 2 + core) * 4 + x) * 2 + yhi) * 8 + z


def shift_perm(major, s):
    pairs = []
    for ylo, core, x, yhi, z in itertools.product(*map(range, SIZES)):
        if (core == 0) == major:
            source = flat(ylo, core, (x + s) % 4, yhi, z)
        else:
            y = (2 * yhi + ylo + s) % 4
            source = flat(y % 2, core, x, y // 2, z)
        pairs.append((source, flat(ylo, core, x, yhi, z)))
    return pairs


def from_major(v, s):
    return lax.ppermute(v, AXES, shift_perm(True, s))


def from_minor(v, s):
    return lax.ppermute(v, AXES, shift_perm(False, s))


def from_z(v, s):
    return lax.ppermute(v, "z", [((i + s) % NZ, i) for i in range(NZ)])


def z_pair(v):
    return lax.ppermute(v, "z", [(i, i ^ 1) for i in range(NZ)])


def sibling(v):
    return lax.ppermute(v, "core", [(0, 1), (1, 0)])


def dot_t(a, b):
    return lax.dot_general(a, b, (((0,), (0,)), ((), ())), preferred_element_type=F32)


def place(at, i, j, other):
    across = (at[2] == 0) != bool(other)
    dx, dy = jnp.where(across, i, j), jnp.where(across, j, i)
    block = lax.rem(at[0] + dx, 4) * 2 + lax.div(lax.rem(at[1] + dy, 4), 2)
    return block, lax.rem(dy, 2)


OWN = ((0, 0), (0, 1), (0, 2), (0, 3))
THROUGH = ((1, 0), (1, 1), (3, 2), (3, 3))
DIRECT = ((1, 2), (1, 3), (3, 0), (3, 1))
FAR = ((2, 0), (2, 1), (2, 2), (2, 3))


def block_at(at, blocks, t, other):
    def select(values):
        out = jnp.int32(values[0])
        for k, v in enumerate(values[1:], 1):
            out = jnp.where(t == k, v, out)
        return out

    i, j = zip(*blocks)
    return place(at, select(i), select(j), other)


def half_specs(rows, n):
    def spec(k):
        return pl.BlockSpec((1, rows, COLS), lambda t, at: (jnp.clip(t - 2 * k, 0, 1), 0, 0))

    return [spec(k) for k in range(n)]


def hidden_kernel(blocks, first, last, at, wg0, wu0, wg1, wu1, *refs):
    t, n = pl.program_id(0), len(blocks) // 2
    own, theirs, refs = refs[:n], refs[n : 2 * n], refs[2 * n :]
    if not first:
        before, refs = refs[0], refs[1:]
    if last:
        w_ref, h_ref, acc = refs
    else:
        (acc,) = refs

    @pl.when(t == 0)
    def _():
        acc[...] = jnp.zeros_like(acc) if first else before[...]

    for k, pair in enumerate(zip(own, theirs)):

        @pl.when(lax.div(t, 2) == k)
        def _(pair=pair):
            for part, (ref, wg, wu) in enumerate(zip(pair, (wg0, wg1), (wu0, wu1))):
                _, group = block_at(at, blocks, t, part)
                v = ref[0]
                acc[part, group, 0] += dot_t(wg[...], v)
                acc[part, group, 1] += dot_t(wu[...], v)

    if last:

        @pl.when(t == len(blocks) - 1)
        def _():
            for part in range(2):
                for group in range(2):
                    g, u = acc[part, group, 0], acc[part, group, 1]
                    h = g / (1.0 + jnp.exp(-g)) * u * w_ref[part, group]
                    h_ref[part, group] = h.astype(BF16)


def hidden_of(at, wg, wu, blocks, own, theirs, before=None, w=None):
    d, ff = wg.shape
    rows = d // 8
    sums = (2, 2, 2, ff, COLS)

    def weights(part):
        return pl.BlockSpec((rows, ff), lambda t, at: (block_at(at, blocks, t, part)[0], 0))

    whole = lambda shape: pl.BlockSpec(shape, lambda t, at: (0,) * len(shape))
    in_specs = [weights(0)] * 2 + [weights(1)] * 2 + half_specs(rows, len(own)) * 2
    args = [wg, wu, wg, wu, *own, *theirs]
    if before is not None:
        in_specs.append(whole(sums))
        args.append(before)
    if w is not None:
        in_specs.append(whole((2, 2, 1, COLS)))
        args.append(w)
        out = (2, 2, ff, COLS)
        out_specs, out_shape = whole(out), jax.ShapeDtypeStruct(out, BF16)
        scratch = [pltpu.VMEM(sums, F32)]
    else:
        out_specs, out_shape, scratch = whole(sums), jax.ShapeDtypeStruct(sums, F32), []

    def kernel(*refs):
        hidden_kernel(blocks, before is None, w is not None, *refs)

    return pl.pallas_call(
        kernel,
        grid_spec=pltpu.PrefetchScalarGridSpec(
            num_scalar_prefetch=1,
            grid=(len(blocks),),
            in_specs=in_specs,
            out_specs=out_specs,
            scratch_shapes=scratch,
        ),
        out_shape=out_shape,
        compiler_params=pltpu.CompilerParams(vmem_limit_bytes=24 * 1024 * 1024),
    )(at, *args)


def down_kernel(keep, via_n, at, wd0, wd1, h0, h1, *refs):
    t = pl.program_id(0)
    for e, (wd, h) in enumerate(((wd0, h0), (wd1, h1))):
        o = dot_t(wd[...], h[0, 0])
        if not keep:
            refs[0][e] = o.astype(BF16)
            continue
        o = o + refs[0][e].astype(F32)
        outs = refs[1 + via_n :]
        for k in range(2):

            @pl.when(t == k)
            def _(k=k, o=o):
                if via_n:
                    outs[2 * k + e][0] = (o + refs[1 + k][e].astype(F32)).astype(BF16)
                else:
                    outs[k][e] = o.astype(BF16)


def down_of(at, wd, h, blocks, got=None, first=0, via=()):
    ff, d = wd.shape
    rows = d // 8
    part = 1 if got is None else 0
    pair = pl.BlockSpec((2, rows, COLS), lambda t, at: (t + first // 2, 0, 0))
    still = lambda n: pl.BlockSpec((n, rows, COLS), lambda t, at: (0, 0, 0))

    def weights(e):
        return pl.BlockSpec((ff, rows), lambda t, at: (0, block_at(at, blocks, 2 * t + e, part)[0]))

    def units(e):
        return pl.BlockSpec((1, 1, ff, COLS), lambda t, at: (part, block_at(at, blocks, 2 * t + e, part)[1], 0, 0))

    in_specs = [weights(0), weights(1), units(0), units(1)]
    args = [wd, wd, h, h]
    if got is None:
        out_specs, out_shape = pair, jax.ShapeDtypeStruct((len(blocks), rows, COLS), BF16)
    else:
        in_specs += [pair] + [still(2)] * len(via)
        args += [got, *via]
        n = 1 if via else 2
        out_specs, out_shape = [still(n)] * (4 // n), [jax.ShapeDtypeStruct((n, rows, COLS), BF16)] * (4 // n)

    def kernel(*refs):
        down_kernel(got is not None, len(via), *refs)

    return pl.pallas_call(
        kernel,
        grid_spec=pltpu.PrefetchScalarGridSpec(
            num_scalar_prefetch=1, grid=(len(blocks) // 2,), in_specs=in_specs, out_specs=out_specs
        ),
        out_shape=out_shape,
        compiler_params=pltpu.CompilerParams(vmem_limit_bytes=16 * 1024 * 1024),
    )(at, *args)


def join_kernel(a, b, c, d, low, high):
    for out, pair in ((low, (a, b)), (high, (c, d))):
        for i, v in enumerate(pair):
            out[i] = v[...]


def join(*pieces):
    out = jax.ShapeDtypeStruct((2, *pieces[0].shape), BF16)
    return pl.pallas_call(
        join_kernel,
        out_shape=[out, out],
        compiler_params=pltpu.CompilerParams(vmem_limit_bytes=10 * 1024 * 1024),
    )(*pieces)


def at_index(i, ndim):
    return (jnp.asarray(i, jnp.int32),) + (jnp.int32(0),) * (ndim - 1)


def put(buf, piece, i):
    return lax.dynamic_update_slice(buf, piece, at_index(i, buf.ndim))


def take(buf, i):
    return lax.dynamic_slice(buf, at_index(i, buf.ndim), (1,) + buf.shape[1:])[0]


def total(*vs):
    out = vs[0].astype(F32)
    for v in vs[1:]:
        out = out + v.astype(F32)
    return out.astype(BF16)


def body(tokens, expert_ids, route_gates, w_gate, w_up, w_down):
    feats = tokens.shape[1]
    rows = NZ * feats
    ylo, core, x, yhi, z = (lax.axis_index(a).astype(jnp.int32) for a in AXES)
    zh, zl = z // 2, z % 2
    at = jnp.stack([x, 2 * yhi + ylo, core])
    wg, wu, wd = w_gate[0], w_up[0], w_down[0]

    own = tokens.T
    quad = jnp.zeros((NZ // 2, feats, COLS), BF16)
    for s in range(NZ // 2):
        quad = put(quad, (from_z(own, 2 * s) if s else own)[None], (zh + s) % 4)
    pair = z_pair(quad)
    start = jnp.stack([jnp.where(zl == 0, quad, pair), jnp.where(zl == 0, pair, quad)], axis=1)
    start = start.reshape(rows, COLS)

    experts = jnp.arange(4, dtype=jnp.int32)
    mine = jnp.sum(
        jnp.where(expert_ids[None, :, :] == experts[:, None, None], route_gates[None], 0.0), axis=2
    )
    near = jnp.stack([mine, sibling(mine)])
    other = lax.ppermute(near, "ylo", [(0, 1), (1, 0)])
    w = jnp.stack([near, other], axis=1)
    w = lax.dynamic_index_in_dim(w, 2 * ylo + core, axis=2)

    steps = {s: from_minor(start, s) for s in (1, 2, 3)}
    own = join(start, steps[1], steps[2], steps[3])

    through = [from_major(own[0], 1), from_major(own[1], 3)]
    direct = [from_major(own[1], 1), from_major(own[0], 3)]
    far = [from_major(through[0], 1), from_major(through[1], 3)]
    swap = lambda vs: [sibling(v) for v in vs]
    sums = hidden_of(at, wg, wu, OWN, own, swap(own))
    *direct, sums, w = lax.optimization_barrier((*direct, sums, w))
    near = [*through, *direct]
    sums = hidden_of(at, wg, wu, THROUGH + DIRECT, near, swap(near), sums)
    *far, sums = lax.optimization_barrier((*far, sums))
    h = hidden_of(at, wg, wu, FAR, far, swap(far), sums, w)

    def after(h, v):
        return lax.optimization_barrier((h, v))

    h, p = after(h, down_of(at, wd, h, FAR))
    got = sibling(p)
    h, give, rest = lax.optimization_barrier((h, down_of(at, wd, h, DIRECT), down_of(at, wd, h, THROUGH + OWN)))
    h, got = after(h, got)
    far = down_of(at, wd, h, FAR, got)
    h, give, rest, *far = lax.optimization_barrier((h, give, rest, *far))
    via = [from_major(far[0], 3), from_major(far[1], 1)]
    h, got = after(h, sibling(give))
    direct = down_of(at, wd, h, DIRECT, got)
    direct = [from_major(direct[0], 3), from_major(direct[1], 1)]
    got = sibling(rest)
    h, through = after(h, down_of(at, wd, h, THROUGH, got, 0, via))
    through = [from_major(v, s) for v, s in zip(through, (3, 3, 1, 1))]
    own = down_of(at, wd, h, OWN, got, 4)
    low = [total(own[0][j], through[j][0], direct[1][j]) for j in range(2)]
    high = [total(own[1][j], direct[0][j], through[2 + j][0]) for j in range(2)]

    c = [*low, *high]
    came = {s: from_minor(c[s], -s) for s in (2, 1, 3)}
    c = total(c[0], came[1], came[3], came[2])

    c = c.reshape(NZ // 2, 2, feats, COLS)
    half = lambda i: lax.dynamic_index_in_dim(c, i, axis=1, keepdims=False)
    quad = total(half(zl), z_pair(half(1 - zl)))
    chunk = lambda s: take(quad, (zh + s) % 4)
    c = total(chunk(0), *[from_z(chunk(s), -2 * s) for s in (2, 1, 3)])
    return c.T


def solution(mesh):
    fine = Mesh(mesh.devices.reshape(SIZES), AXES)
    expert, tensor = ("ylo", "core"), ("x", "yhi", "z")
    in_specs = (
        P(expert, tensor),
        P(expert, None),
        P(expert, None),
        P(expert, None, tensor),
        P(expert, None, tensor),
        P(expert, tensor, None),
    )
    return jax.shard_map(
        body, mesh=fine, in_specs=in_specs, out_specs=P(expert, tensor), check_vma=False
    )
```

```python
import itertools

import jax
import jax.numpy as jnp
from jax import lax
from jax.experimental import pallas as pl
from jax.experimental.pallas import tpu as pltpu
from jax.sharding import Mesh, PartitionSpec as P

AXES = ("ylo", "core", "x", "yhi", "z")
SIZES = (2, 2, 4, 2, 8)
NZ = 8
BF16, F32 = jnp.bfloat16, jnp.float32
COLS = 256


def flat(ylo, core, x, yhi, z):
    return (((ylo * 2 + core) * 4 + x) * 2 + yhi) * 8 + z


def shift_perm(major, s):
    pairs = []
    for ylo, core, x, yhi, z in itertools.product(*map(range, SIZES)):
        if (core == 0) == major:
            source = flat(ylo, core, (x + s) % 4, yhi, z)
        else:
            y = (2 * yhi + ylo + s) % 4
            source = flat(y % 2, core, x, y // 2, z)
        pairs.append((source, flat(ylo, core, x, yhi, z)))
    return pairs


def from_major(v, s):
    return lax.ppermute(v, AXES, shift_perm(True, s))


def from_minor(v, s):
    return lax.ppermute(v, AXES, shift_perm(False, s))


def from_z(v, s):
    return lax.ppermute(v, "z", [((i + s) % NZ, i) for i in range(NZ)])


def z_pair(v):
    return lax.ppermute(v, "z", [(i, i ^ 1) for i in range(NZ)])


def sibling(v):
    return lax.ppermute(v, "core", [(0, 1), (1, 0)])


def dot_t(a, b):
    return lax.dot_general(a, b, (((0,), (0,)), ((), ())), preferred_element_type=F32)


def place(at, i, j, other):
    across = (at[2] == 0) != bool(other)
    dx, dy = jnp.where(across, i, j), jnp.where(across, j, i)
    block = lax.rem(at[0] + dx, 4) * 2 + lax.div(lax.rem(at[1] + dy, 4), 2)
    return block, lax.rem(dy, 2)


OWN = ((0, 0), (0, 1), (0, 2), (0, 3))
THROUGH = ((1, 0), (1, 1), (3, 2), (3, 3))
DIRECT = ((1, 2), (1, 3), (3, 0), (3, 1))
FAR = ((2, 0), (2, 1), (2, 2), (2, 3))


def block_at(at, blocks, t, other):
    def select(values):
        out = jnp.int32(values[0])
        for k, v in enumerate(values[1:], 1):
            out = jnp.where(t == k, v, out)
        return out

    i, j = zip(*blocks)
    return place(at, select(i), select(j), other)


def half_specs(rows, n):
    def spec(k):
        return pl.BlockSpec((1, rows, COLS), lambda t, at: (jnp.clip(t - 2 * k, 0, 1), 0, 0))

    return [spec(k) for k in range(n)]


def hidden_kernel(blocks, first, last, at, wg0, wu0, wg1, wu1, *refs):
    t, n = pl.program_id(0), len(blocks) // 2
    own, theirs, refs = refs[:n], refs[n : 2 * n], refs[2 * n :]
    if not first:
        before, refs = refs[0], refs[1:]
    if last:
        w_ref, h_ref, acc = refs
    else:
        (acc,) = refs

    @pl.when(t == 0)
    def _():
        acc[...] = jnp.zeros_like(acc) if first else before[...]

    for k, pair in enumerate(zip(own, theirs)):

        @pl.when(lax.div(t, 2) == k)
        def _(pair=pair):
            for part, (ref, wg, wu) in enumerate(zip(pair, (wg0, wg1), (wu0, wu1))):
                _, group = block_at(at, blocks, t, part)
                v = ref[0]
                acc[part, group, 0] += dot_t(wg[...], v)
                acc[part, group, 1] += dot_t(wu[...], v)

    if last:

        @pl.when(t == len(blocks) - 1)
        def _():
            for part in range(2):
                for group in range(2):
                    g, u = acc[part, group, 0], acc[part, group, 1]
                    h = g / (1.0 + jnp.exp(-g)) * u * w_ref[part, group]
                    h_ref[part, group] = h.astype(BF16)


def hidden_of(at, wg, wu, blocks, own, theirs, before=None, w=None):
    d, ff = wg.shape
    rows = d // 8
    sums = (2, 2, 2, ff, COLS)

    def weights(part):
        return pl.BlockSpec((rows, ff), lambda t, at: (block_at(at, blocks, t, part)[0], 0))

    whole = lambda shape: pl.BlockSpec(shape, lambda t, at: (0,) * len(shape))
    in_specs = [weights(0)] * 2 + [weights(1)] * 2 + half_specs(rows, len(own)) * 2
    args = [wg, wu, wg, wu, *own, *theirs]
    if before is not None:
        in_specs.append(whole(sums))
        args.append(before)
    if w is not None:
        in_specs.append(whole((2, 2, 1, COLS)))
        args.append(w)
        out = (2, 2, ff, COLS)
        out_specs, out_shape = whole(out), jax.ShapeDtypeStruct(out, BF16)
        scratch = [pltpu.VMEM(sums, F32)]
    else:
        out_specs, out_shape, scratch = whole(sums), jax.ShapeDtypeStruct(sums, F32), []

    def kernel(*refs):
        hidden_kernel(blocks, before is None, w is not None, *refs)

    return pl.pallas_call(
        kernel,
        grid_spec=pltpu.PrefetchScalarGridSpec(
            num_scalar_prefetch=1,
            grid=(len(blocks),),
            in_specs=in_specs,
            out_specs=out_specs,
            scratch_shapes=scratch,
        ),
        out_shape=out_shape,
        compiler_params=pltpu.CompilerParams(vmem_limit_bytes=24 * 1024 * 1024),
    )(at, *args)


def down_kernel(keep, via_n, at, wd_ref, h_ref, *refs):
    t = pl.program_id(0)
    o = dot_t(wd_ref[...], h_ref[0, 0])
    if not keep:
        refs[0][0] = o.astype(BF16)
        return
    o = o + refs[0][0].astype(F32)
    if via_n:
        via, outs = refs[1 : 1 + via_n], refs[1 + via_n :]
        o = o + jnp.where(t < 2, via[0][0], via[1][0]).astype(F32)
        for k, ref in enumerate(outs):

            @pl.when(t == k)
            def _(ref=ref):
                ref[0] = o.astype(BF16)

        return
    for k, ref in enumerate(refs[1:]):

        @pl.when(lax.div(t, 2) == k)
        def _(ref=ref):
            ref[0] = o.astype(BF16)


def down_of(at, wd, h, blocks, got=None, first=0, via=()):
    ff, d = wd.shape
    rows = d // 8
    part = 1 if got is None else 0
    whole = pl.BlockSpec((1, rows, COLS), lambda t, at: (t + first, 0, 0))
    in_specs = [
        pl.BlockSpec((ff, rows), lambda t, at: (0, block_at(at, blocks, t, part)[0])),
        pl.BlockSpec((1, 1, ff, COLS), lambda t, at: (part, block_at(at, blocks, t, part)[1], 0, 0)),
    ]
    args = [wd, h]
    if got is None:
        out_specs, out_shape = whole, jax.ShapeDtypeStruct((len(blocks), rows, COLS), BF16)
    else:
        in_specs += [whole, *half_specs(rows, len(via))]
        args += [got, *via]
        out_specs, out_shape = half_specs(rows, 2), [jax.ShapeDtypeStruct((2, rows, COLS), BF16)] * 2
        if via:
            out_specs = [pl.BlockSpec((1, rows, COLS), lambda t, at: (0, 0, 0))] * 4
            out_shape = [jax.ShapeDtypeStruct((1, rows, COLS), BF16)] * 4

    def kernel(*refs):
        down_kernel(got is not None, len(via), *refs)

    return pl.pallas_call(
        kernel,
        grid_spec=pltpu.PrefetchScalarGridSpec(
            num_scalar_prefetch=1, grid=(len(blocks),), in_specs=in_specs, out_specs=out_specs
        ),
        out_shape=out_shape,
        compiler_params=pltpu.CompilerParams(vmem_limit_bytes=12 * 1024 * 1024),
    )(at, *args)


def join_kernel(a, b, c, d, low, high):
    for out, pair in ((low, (a, b)), (high, (c, d))):
        for i, v in enumerate(pair):
            out[i] = v[...]


def join(*pieces):
    out = jax.ShapeDtypeStruct((2, *pieces[0].shape), BF16)
    return pl.pallas_call(
        join_kernel,
        out_shape=[out, out],
        compiler_params=pltpu.CompilerParams(vmem_limit_bytes=10 * 1024 * 1024),
    )(*pieces)


def at_index(i, ndim):
    return (jnp.asarray(i, jnp.int32),) + (jnp.int32(0),) * (ndim - 1)


def put(buf, piece, i):
    return lax.dynamic_update_slice(buf, piece, at_index(i, buf.ndim))


def take(buf, i):
    return lax.dynamic_slice(buf, at_index(i, buf.ndim), (1,) + buf.shape[1:])[0]


def total(*vs):
    out = vs[0].astype(F32)
    for v in vs[1:]:
        out = out + v.astype(F32)
    return out.astype(BF16)


def body(tokens, expert_ids, route_gates, w_gate, w_up, w_down):
    feats = tokens.shape[1]
    rows = NZ * feats
    ylo, core, x, yhi, z = (lax.axis_index(a).astype(jnp.int32) for a in AXES)
    zh, zl = z // 2, z % 2
    at = jnp.stack([x, 2 * yhi + ylo, core])
    wg, wu, wd = w_gate[0], w_up[0], w_down[0]

    own = tokens.T
    quad = jnp.zeros((NZ // 2, feats, COLS), BF16)
    for s in range(NZ // 2):
        quad = put(quad, (from_z(own, 2 * s) if s else own)[None], (zh + s) % 4)
    pair = z_pair(quad)
    start = jnp.stack([jnp.where(zl == 0, quad, pair), jnp.where(zl == 0, pair, quad)], axis=1)
    start = start.reshape(rows, COLS)

    experts = jnp.arange(4, dtype=jnp.int32)
    mine = jnp.sum(
        jnp.where(expert_ids[None, :, :] == experts[:, None, None], route_gates[None], 0.0), axis=2
    )
    near = jnp.stack([mine, sibling(mine)])
    other = lax.ppermute(near, "ylo", [(0, 1), (1, 0)])
    w = jnp.stack([near, other], axis=1)
    w = lax.dynamic_index_in_dim(w, 2 * ylo + core, axis=2)

    steps = {s: from_minor(start, s) for s in (1, 2, 3)}
    own = join(start, steps[1], steps[2], steps[3])

    through = [from_major(own[0], 1), from_major(own[1], 3)]
    direct = [from_major(own[1], 1), from_major(own[0], 3)]
    far = [from_major(through[0], 1), from_major(through[1], 3)]
    swap = lambda vs: [sibling(v) for v in vs]
    sums = hidden_of(at, wg, wu, OWN, own, swap(own))
    *direct, sums, w = lax.optimization_barrier((*direct, sums, w))
    near = [*through, *direct]
    sums = hidden_of(at, wg, wu, THROUGH + DIRECT, near, swap(near), sums)
    *far, sums = lax.optimization_barrier((*far, sums))
    h = hidden_of(at, wg, wu, FAR, far, swap(far), sums, w)

    def after(h, v):
        return lax.optimization_barrier((h, v))

    h, p = after(h, down_of(at, wd, h, FAR))
    got = sibling(p)
    h, give, rest = lax.optimization_barrier((h, down_of(at, wd, h, DIRECT), down_of(at, wd, h, THROUGH + OWN)))
    h, got = after(h, got)
    far = down_of(at, wd, h, FAR, got)
    h, give, rest, *far = lax.optimization_barrier((h, give, rest, *far))
    via = [from_major(far[0], 3), from_major(far[1], 1)]
    h, got = after(h, sibling(give))
    direct = down_of(at, wd, h, DIRECT, got)
    direct = [from_major(direct[0], 3), from_major(direct[1], 1)]
    got = sibling(rest)
    h, through = after(h, down_of(at, wd, h, THROUGH, got, 0, via))
    through = [from_major(v, s) for v, s in zip(through, (3, 3, 1, 1))]
    own = down_of(at, wd, h, OWN, got, 4)
    low = [total(own[0][j], through[j][0], direct[1][j]) for j in range(2)]
    high = [total(own[1][j], direct[0][j], through[2 + j][0]) for j in range(2)]

    c = [*low, *high]
    came = {s: from_minor(c[s], -s) for s in (2, 1, 3)}
    c = total(c[0], came[1], came[3], came[2])

    c = c.reshape(NZ // 2, 2, feats, COLS)
    half = lambda i: lax.dynamic_index_in_dim(c, i, axis=1, keepdims=False)
    quad = total(half(zl), z_pair(half(1 - zl)))
    chunk = lambda s: take(quad, (zh + s) % 4)
    c = total(chunk(0), *[from_z(chunk(s), -2 * s) for s in (2, 1, 3)])
    return c.T


def solution(mesh):
    fine = Mesh(mesh.devices.reshape(SIZES), AXES)
    expert, tensor = ("ylo", "core"), ("x", "yhi", "z")
    in_specs = (
        P(expert, tensor),
        P(expert, None),
        P(expert, None),
        P(expert, None, tensor),
        P(expert, None, tensor),
        P(expert, tensor, None),
    )
    return jax.shard_map(
        body, mesh=fine, in_specs=in_specs, out_specs=P(expert, tensor), check_vma=False
    )
```

```python
import itertools

import jax
import jax.numpy as jnp
from jax import lax
from jax.experimental import pallas as pl
from jax.experimental.pallas import tpu as pltpu
from jax.sharding import Mesh, PartitionSpec as P

AXES = ("ylo", "core", "x", "yhi", "z")
SIZES = (2, 2, 4, 2, 8)
NZ = 8
BF16, F32 = jnp.bfloat16, jnp.float32
COLS = 256


def flat(ylo, core, x, yhi, z):
    return (((ylo * 2 + core) * 4 + x) * 2 + yhi) * 8 + z


def shift_perm(major, s):
    pairs = []
    for ylo, core, x, yhi, z in itertools.product(*map(range, SIZES)):
        if (core == 0) == major:
            source = flat(ylo, core, (x + s) % 4, yhi, z)
        else:
            y = (2 * yhi + ylo + s) % 4
            source = flat(y % 2, core, x, y // 2, z)
        pairs.append((source, flat(ylo, core, x, yhi, z)))
    return pairs


def from_major(v, s):
    return lax.ppermute(v, AXES, shift_perm(True, s))


def from_minor(v, s):
    return lax.ppermute(v, AXES, shift_perm(False, s))


def from_z(v, s):
    return lax.ppermute(v, "z", [((i + s) % NZ, i) for i in range(NZ)])


def z_pair(v):
    return lax.ppermute(v, "z", [(i, i ^ 1) for i in range(NZ)])


def sibling(v):
    return lax.ppermute(v, "core", [(0, 1), (1, 0)])


def dot_t(a, b):
    return lax.dot_general(a, b, (((0,), (0,)), ((), ())), preferred_element_type=F32)


def place(at, i, j, other):
    across = (at[2] == 0) != bool(other)
    dx, dy = jnp.where(across, i, j), jnp.where(across, j, i)
    block = lax.rem(at[0] + dx, 4) * 2 + lax.div(lax.rem(at[1] + dy, 4), 2)
    return block, lax.rem(dy, 2)


OWN = ((0, 0), (0, 1), (0, 2), (0, 3))
THROUGH = ((1, 0), (1, 1), (3, 2), (3, 3))
DIRECT = ((1, 2), (1, 3), (3, 0), (3, 1))
FAR = ((2, 0), (2, 1), (2, 2), (2, 3))


def block_at(at, blocks, t, other):
    def select(values):
        out = jnp.int32(values[0])
        for k, v in enumerate(values[1:], 1):
            out = jnp.where(t == k, v, out)
        return out

    i, j = zip(*blocks)
    return place(at, select(i), select(j), other)


def half_specs(rows, n):
    def spec(k):
        return pl.BlockSpec((1, rows, COLS), lambda t, at: (jnp.clip(t - 2 * k, 0, 1), 0, 0))

    return [spec(k) for k in range(n)]


def hidden_kernel(blocks, first, last, at, wg0, wu0, wg1, wu1, *refs):
    t, n = pl.program_id(0), len(blocks) // 2
    own, theirs, refs = refs[:n], refs[n : 2 * n], refs[2 * n :]
    if not first:
        before, refs = refs[0], refs[1:]
    if last:
        w_ref, h_ref, acc = refs
    else:
        (acc,) = refs

    @pl.when(t == 0)
    def _():
        acc[...] = jnp.zeros_like(acc) if first else before[...]

    for k, pair in enumerate(zip(own, theirs)):

        @pl.when(lax.div(t, 2) == k)
        def _(pair=pair):
            for part, (ref, wg, wu) in enumerate(zip(pair, (wg0, wg1), (wu0, wu1))):
                _, group = block_at(at, blocks, t, part)
                v = ref[0]
                acc[part, group, 0] += dot_t(wg[...], v)
                acc[part, group, 1] += dot_t(wu[...], v)

    if last:

        @pl.when(t == len(blocks) - 1)
        def _():
            for part in range(2):
                for group in range(2):
                    g, u = acc[part, group, 0], acc[part, group, 1]
                    h = g / (1.0 + jnp.exp(-g)) * u * w_ref[part, group]
                    h_ref[part, group] = h.astype(BF16)


def hidden_of(at, wg, wu, blocks, own, theirs, before=None, w=None):
    d, ff = wg.shape
    rows = d // 8
    sums = (2, 2, 2, ff, COLS)

    def weights(part):
        return pl.BlockSpec((rows, ff), lambda t, at: (block_at(at, blocks, t, part)[0], 0))

    whole = lambda shape: pl.BlockSpec(shape, lambda t, at: (0,) * len(shape))
    in_specs = [weights(0)] * 2 + [weights(1)] * 2 + half_specs(rows, len(own)) * 2
    args = [wg, wu, wg, wu, *own, *theirs]
    if before is not None:
        in_specs.append(whole(sums))
        args.append(before)
    if w is not None:
        in_specs.append(whole((2, 2, 1, COLS)))
        args.append(w)
        out = (2, 2, ff, COLS)
        out_specs, out_shape = whole(out), jax.ShapeDtypeStruct(out, BF16)
        scratch = [pltpu.VMEM(sums, F32)]
    else:
        out_specs, out_shape, scratch = whole(sums), jax.ShapeDtypeStruct(sums, F32), []

    def kernel(*refs):
        hidden_kernel(blocks, before is None, w is not None, *refs)

    return pl.pallas_call(
        kernel,
        grid_spec=pltpu.PrefetchScalarGridSpec(
            num_scalar_prefetch=1,
            grid=(len(blocks),),
            in_specs=in_specs,
            out_specs=out_specs,
            scratch_shapes=scratch,
        ),
        out_shape=out_shape,
        compiler_params=pltpu.CompilerParams(vmem_limit_bytes=24 * 1024 * 1024),
    )(at, *args)


def down_kernel(keep, via_n, at, wd_ref, h_ref, *refs):
    t = pl.program_id(0)
    o = dot_t(wd_ref[...], h_ref[0, 0])
    if not keep:
        refs[0][0] = o.astype(BF16)
        return
    o = o + refs[0][0].astype(F32)
    if via_n:
        via, outs = refs[1 : 1 + via_n], refs[1 + via_n :]
        o = o + jnp.where(t < 2, via[0][0], via[1][0]).astype(F32)
        for k, ref in enumerate(outs):

            @pl.when(t == k)
            def _(ref=ref):
                ref[0] = o.astype(BF16)

        return
    for k, ref in enumerate(refs[1:]):

        @pl.when(lax.div(t, 2) == k)
        def _(ref=ref):
            ref[0] = o.astype(BF16)


def down_of(at, wd, h, blocks, got=None, first=0, via=()):
    ff, d = wd.shape
    rows = d // 8
    part = 1 if got is None else 0
    whole = pl.BlockSpec((1, rows, COLS), lambda t, at: (t + first, 0, 0))
    in_specs = [
        pl.BlockSpec((ff, rows), lambda t, at: (0, block_at(at, blocks, t, part)[0])),
        pl.BlockSpec((1, 1, ff, COLS), lambda t, at: (part, block_at(at, blocks, t, part)[1], 0, 0)),
    ]
    args = [wd, h]
    if got is None:
        out_specs, out_shape = whole, jax.ShapeDtypeStruct((len(blocks), rows, COLS), BF16)
    else:
        in_specs += [whole, *half_specs(rows, len(via))]
        args += [got, *via]
        out_specs, out_shape = half_specs(rows, 2), [jax.ShapeDtypeStruct((2, rows, COLS), BF16)] * 2
        if via:
            out_specs = [pl.BlockSpec((1, rows, COLS), lambda t, at: (0, 0, 0))] * 4
            out_shape = [jax.ShapeDtypeStruct((1, rows, COLS), BF16)] * 4

    def kernel(*refs):
        down_kernel(got is not None, len(via), *refs)

    return pl.pallas_call(
        kernel,
        grid_spec=pltpu.PrefetchScalarGridSpec(
            num_scalar_prefetch=1, grid=(len(blocks),), in_specs=in_specs, out_specs=out_specs
        ),
        out_shape=out_shape,
        compiler_params=pltpu.CompilerParams(vmem_limit_bytes=12 * 1024 * 1024),
    )(at, *args)


def join_kernel(a, b, c, d, low, high):
    for out, pair in ((low, (a, b)), (high, (c, d))):
        for i, v in enumerate(pair):
            out[i] = v[...]


def join(*pieces):
    out = jax.ShapeDtypeStruct((2, *pieces[0].shape), BF16)
    return pl.pallas_call(
        join_kernel,
        out_shape=[out, out],
        compiler_params=pltpu.CompilerParams(vmem_limit_bytes=10 * 1024 * 1024),
    )(*pieces)


def at_index(i, ndim):
    return (jnp.asarray(i, jnp.int32),) + (jnp.int32(0),) * (ndim - 1)


def put(buf, piece, i):
    return lax.dynamic_update_slice(buf, piece, at_index(i, buf.ndim))


def take(buf, i):
    return lax.dynamic_slice(buf, at_index(i, buf.ndim), (1,) + buf.shape[1:])[0]


def total(*vs):
    out = vs[0].astype(F32)
    for v in vs[1:]:
        out = out + v.astype(F32)
    return out.astype(BF16)


def body(tokens, expert_ids, route_gates, w_gate, w_up, w_down):
    feats = tokens.shape[1]
    rows = NZ * feats
    ylo, core, x, yhi, z = (lax.axis_index(a).astype(jnp.int32) for a in AXES)
    zh, zl = z // 2, z % 2
    at = jnp.stack([x, 2 * yhi + ylo, core])
    wg, wu, wd = w_gate[0], w_up[0], w_down[0]

    own = tokens.T
    quad = jnp.zeros((NZ // 2, feats, COLS), BF16)
    for s in range(NZ // 2):
        quad = put(quad, (from_z(own, 2 * s) if s else own)[None], (zh + s) % 4)
    pair = z_pair(quad)
    start = jnp.stack([jnp.where(zl == 0, quad, pair), jnp.where(zl == 0, pair, quad)], axis=1)
    start = start.reshape(rows, COLS)

    experts = jnp.arange(4, dtype=jnp.int32)
    mine = jnp.sum(
        jnp.where(expert_ids[None, :, :] == experts[:, None, None], route_gates[None], 0.0), axis=2
    )
    near = jnp.stack([mine, sibling(mine)])
    other = lax.ppermute(near, "ylo", [(0, 1), (1, 0)])
    w = jnp.stack([near, other], axis=1)
    w = lax.dynamic_index_in_dim(w, 2 * ylo + core, axis=2)

    steps = {s: from_minor(start, s) for s in (1, 2, 3)}
    own = join(start, steps[1], steps[2], steps[3])

    *own, w = lax.optimization_barrier((*own, w))

    through = [from_major(own[0], 1), from_major(own[1], 3)]
    direct = [from_major(own[1], 1), from_major(own[0], 3)]
    far = [from_major(through[0], 1), from_major(through[1], 3)]
    swap = lambda vs: [sibling(v) for v in vs]
    sums = hidden_of(at, wg, wu, OWN, own, swap(own))
    *direct, sums = lax.optimization_barrier((*direct, sums))
    near = [*through, *direct]
    sums = hidden_of(at, wg, wu, THROUGH + DIRECT, near, swap(near), sums)
    *far, sums = lax.optimization_barrier((*far, sums))
    h = hidden_of(at, wg, wu, FAR, far, swap(far), sums, w)

    def after(h, v):
        return lax.optimization_barrier((h, v))

    h, p = after(h, down_of(at, wd, h, FAR))
    got = sibling(p)
    h, give, rest = lax.optimization_barrier((h, down_of(at, wd, h, DIRECT), down_of(at, wd, h, THROUGH + OWN)))
    h, got = after(h, got)
    far = down_of(at, wd, h, FAR, got)
    h, give, rest, *far = lax.optimization_barrier((h, give, rest, *far))
    via = [from_major(far[0], 3), from_major(far[1], 1)]
    h, got = after(h, sibling(give))
    direct = down_of(at, wd, h, DIRECT, got)
    direct = [from_major(direct[0], 3), from_major(direct[1], 1)]
    got = sibling(rest)
    h, through = after(h, down_of(at, wd, h, THROUGH, got, 0, via))
    through = [from_major(v, s) for v, s in zip(through, (3, 3, 1, 1))]
    own = down_of(at, wd, h, OWN, got, 4)
    low = [total(own[0][j], through[j][0], direct[1][j]) for j in range(2)]
    high = [total(own[1][j], direct[0][j], through[2 + j][0]) for j in range(2)]

    c = [*low, *high]
    came = {s: from_minor(c[s], -s) for s in (2, 1, 3)}
    c = total(c[0], came[1], came[3], came[2])

    c = c.reshape(NZ // 2, 2, feats, COLS)
    half = lambda i: lax.dynamic_index_in_dim(c, i, axis=1, keepdims=False)
    quad = total(half(zl), z_pair(half(1 - zl)))
    chunk = lambda s: take(quad, (zh + s) % 4)
    c = total(chunk(0), *[from_z(chunk(s), -2 * s) for s in (2, 1, 3)])
    return c.T


def solution(mesh):
    fine = Mesh(mesh.devices.reshape(SIZES), AXES)
    expert, tensor = ("ylo", "core"), ("x", "yhi", "z")
    in_specs = (
        P(expert, tensor),
        P(expert, None),
        P(expert, None),
        P(expert, None, tensor),
        P(expert, None, tensor),
        P(expert, tensor, None),
    )
    return jax.shard_map(
        body, mesh=fine, in_specs=in_specs, out_specs=P(expert, tensor), check_vma=False
    )
```
